1024 devices in a mesh: gx: 8 (over y_hi, core), gy: 8 (over z), gz: 16 (over y_lo, x).
Axes of the slice: x: 8, y: 8 (y_hi: 4, y_lo: 2; y = y_hi * 2 + y_lo), z: 8, core: 2. Of those that a mesh axis runs over, the one named last changes fastest.
Arguments:
- conc: float32 [2, 128, 256, 1024], P(None, 'gz', 'gx', 'gy'), may hold values from -4 to 4
- speed: float32 [3, 128, 256, 1024], P(None, 'gz', 'gx', 'gy'), may hold values from 0.02 to 0.15
- rates: float32 [2, 128, 256, 1024], P(None, 'gz', 'gx', 'gy'), may hold values from 0.005 to 0.06
- region: int32 [128, 256, 1024], P('gz', 'gx', 'gy'), may hold values 0 or 1
- flow_signs: int32 [16, 8, 8], P('gz', 'gx', 'gy'), may hold values from 0 to 7
Outputs:
- final: float32 [2, 128, 256, 1024], P(None, 'gz', 'gx', 'gy')
The draws below stay inside these ranges and needn't reach their ends.
Inputs may be any that keep to these rules, and one draw needn't show every extreme that they name: `flow_signs`: bit 0, 1, 2 set: flow toward lower z, x, y in that subdomain.
All inputs are finite; a program needn't handle non-finite values. No bound on the sum of `region` on one device may be relied on, other than what follows from the above.
Results may differ from the reference program's by a relative error of at most 0.000088.
Values sent between devices are 32-bit elements; how exact they have to be, the bound alone decides.
A program may use at most 32 MiB of HBM per device.

```python
import math
import jax
import jax.numpy as jnp
from jax import lax

CZ = 8
CX = 32
CY = 128
NT = 16
ITERS = 3
BLOCKS_Z = 16
BLOCKS_X = 8
BLOCKS_Y = 8
NZ = 128
NX = 256
NY = 1024


def draw_conc(key, part):
    key = jax.random.fold_in(key, 7)
    return jax.random.truncated_normal(key, -4.0, 4.0, (2, NZ, NX, NY), jnp.float32)


def plant(entries, key, smallest, high):
    index_at = [jax.random.randint(jax.random.fold_in(key, axis), (), 0, length) for axis, length in enumerate(entries.shape)]
    main_axis = entries.shape.index(max(entries.shape))
    next_to = index_at[:main_axis] + [(index_at[main_axis] + 1) % entries.shape[main_axis]] + index_at[main_axis + 1:]
    return entries.at[tuple(index_at)].set(smallest).at[tuple(next_to)].set(high)


def levels(rng, dims, split, smallest, high):
    def one(position, blocks):
        draws = jax.random.uniform(jax.random.fold_in(jax.random.fold_in(rng, 6), position), (blocks,), jnp.float32, smallest / len(split), high / len(split))
        return jnp.repeat(jnp.exp(draws), dims[position] // blocks).reshape((-1,) + (1,) * (len(dims) - position - 1))

    gain = one(*split[0])
    for cut in split[1:]:
        gain = gain * one(*cut)
    return gain


def setup_inputs(seed: int = 0) -> dict:
    key_of = jax.random.split(jax.random.key(seed), 6)
    conc = draw_conc(jax.random.fold_in(key_of[5], 71), 0)
    speed = jnp.clip(0.02 + 0.13000001 * jax.random.uniform(key_of[1], (3, NZ, NX, NY), jnp.float32) ** levels(key_of[1], (3, NZ, NX, NY), ((1, 16), (2, 8), (3, 8)), -0.2, 0.2), 0.02, 0.15)
    rates = jnp.clip(jnp.exp(math.log(0.06) - 2.4849066 * jax.random.uniform(key_of[2], (2, NZ, NX, NY), jnp.float32) ** levels(key_of[2], (2, NZ, NX, NY), ((1, 16), (2, 8), (3, 8)), -0.2, 0.2)), 0.005, 0.06)
    region = plant((jax.random.randint(key_of[3], (NZ, NX, NY), 0, 2) < 1).astype(jnp.int32), jax.random.fold_in(key_of[3], 1), 0, 1)
    flow_signs = plant(jax.random.randint(key_of[4], (BLOCKS_Z, BLOCKS_X, BLOCKS_Y), 0, 8), jax.random.fold_in(key_of[4], 1), 0, 7).astype(jnp.int32)
    return dict(conc=conc, speed=speed, rates=rates, region=region, flow_signs=flow_signs)


ROBIN = 0.5
DIFFUSE = 0.07


def layer(field, along, index):
    return lax.index_in_dim(field, index, axis=along, keepdims=False)


def advance(field, ghosts, speeds, rate, region_f, against, axes):
    def neighbours(lower, upper, along):
        padded = jnp.concatenate([jnp.expand_dims(lower, along), field, jnp.expand_dims(upper, along)], axis=along)
        extent = field.shape[along]
        return lax.slice_in_dim(padded, 0, extent, axis=along), lax.slice_in_dim(padded, 2, extent + 2, axis=along)

    lower_z, upper_z = neighbours(ghosts[0], ghosts[1], axes[0])
    lower_x, upper_x = neighbours(ghosts[2], ghosts[3], axes[1])
    lower_y, upper_y = neighbours(ghosts[4], ghosts[5], axes[2])
    total = ((lower_z + upper_z) + (lower_x + upper_x)) + (lower_y + upper_y)
    spread = DIFFUSE * (total - 6.0 * field)
    carry_z = speeds[0] * jnp.where(against[0], field - upper_z, field - lower_z)
    carry_x = speeds[1] * jnp.where(against[1], field - upper_x, field - lower_x)
    carry_y = speeds[2] * jnp.where(against[2], field - upper_y, field - lower_y)
    carried = (carry_z + carry_x) + carry_y
    change = region_f * (rate[1] * field[1] - rate[0] * field[0])
    reaction = jnp.stack([change, -change])
    return field + ((spread - carried) + reaction)


def reference(conc, speed, rates, region, flow_signs):
    shape = (BLOCKS_Z, CZ, BLOCKS_X, CX, BLOCKS_Y, CY)
    start = conc.reshape((2,) + shape)
    speeds = speed.reshape((3,) + shape)
    rate = rates.reshape((2,) + shape)
    region_f = region.astype(jnp.float32).reshape(shape)
    flags = flow_signs.reshape(BLOCKS_Z, 1, BLOCKS_X, 1, BLOCKS_Y, 1)
    against = (flags % 2 == 1, (flags // 2) % 2 == 1, (flags // 4) % 2 == 1)
    axes = (2, 4, 6)
    sizes_here = (CZ, CX, CY)

    def stepper(field, incoming):
        faces = []
        sent = []
        for along, extent in zip(axes, sizes_here):
            faces.append(layer(field, along, 0))
            faces.append(layer(field, along, extent - 1))
            sent.append(layer(field, along, 1) + (ROBIN - 1.0) * layer(field, along, 0))
            sent.append(layer(field, along, extent - 2) + (ROBIN - 1.0) * layer(field, along, extent - 1))
        if incoming is None:
            ghosts = tuple(faces)
        else:
            ghosts = tuple((datum + face) / (1.0 + ROBIN) for datum, face in zip(incoming, faces))
        return advance(field, ghosts, speeds, rate, region_f, against, axes), tuple(sent)

    received = None
    final = start
    for sweep in range(ITERS):
        final, sent = lax.scan(stepper, start, received, length=NT)
        received = (jnp.roll(sent[1], 1, 2), jnp.roll(sent[0], -1, 2),
                    jnp.roll(sent[3], 1, 4), jnp.roll(sent[2], -1, 4),
                    jnp.roll(sent[5], 1, 6), jnp.roll(sent[4], -1, 6))
    return final.reshape(2, NZ, NX, NY)
```

```python
import functools

import jax
import jax.numpy as jnp
from jax import lax
from jax.experimental import pallas as pl
from jax.experimental.pallas import tpu as pltpu
from jax.sharding import PartitionSpec as P

NT = 16
ROBIN = 0.5
DIFFUSE = 0.07
SHARE = 1.0 / (1.0 + ROBIN)

CZ, CX, CY = 8, 32, 128
XT = CX // 8
PAD = CX + 16
FIELD = 2 * CZ * PAD
AXES = ("gz", "gx", "gy")
Z0, Z1, X0, X1, Y0, Y1, SLOT = 0, 64, 128, 144, 160, 176, 192
SLOTS = 2 * (NT - 1)


def kernel(conc, speed, rates, region, flags, out, u, dense, raw, zone, az, ax, ay, cc, kk, send, recv, in_sem, out_sem, send_sem, recv_sem):
    def plane(row, tr, z):
        return row + (tr * CZ + z) * PAD + 8

    get_conc = pltpu.make_async_copy(conc, dense, in_sem.at[0])
    get_conc.start()
    get_speed = pltpu.make_async_copy(speed, raw.at[pl.ds(0, 3)], in_sem.at[1])
    get_rates = pltpu.make_async_copy(rates, raw.at[pl.ds(3, 2)], in_sem.at[2])
    get_region = pltpu.make_async_copy(region, zone, in_sem.at[3])
    get_speed.start()
    get_rates.start()
    get_region.start()

    near = []
    for name in AXES:
        n, me = lax.axis_size(name), lax.axis_index(name)
        near.append(({name: lax.rem(me + n - 1, n)}, {name: lax.rem(me + 1, n)}))
    barrier = pltpu.get_barrier_semaphore()
    for low, high in near:
        pl.semaphore_signal(barrier, inc=1, device_id=low, device_id_type=pl.DeviceIdType.MESH)
        pl.semaphore_signal(barrier, inc=1, device_id=high, device_id_type=pl.DeviceIdType.MESH)

    zero = jnp.zeros((8, CY), jnp.float32)
    for b in range(3):
        for tr in range(2):
            for z in range(CZ):
                u[pl.ds(plane(b * FIELD, tr, z) - 8, 8), :] = zero
                u[pl.ds(plane(b * FIELD, tr, z) + CX, 8), :] = zero

    lane = lax.broadcasted_iota(jnp.int32, (8, CY), 1)
    sub = lax.broadcasted_iota(jnp.int32, (8, CY), 0)
    first, last = lane == 0, lane == CY - 1
    group, place = lane // 4, lane % 4

    get_conc.wait()
    pl.semaphore_wait(barrier, 6)

    def copies(slot):
        result = []
        for src, dst, size, where in (
            (Z0, Z1, 64, near[0][0]),
            (Z1, Z0, 64, near[0][1]),
            (X0, X1, 16, near[1][0]),
            (X1, X0, 16, near[1][1]),
            (Y0, Y1, 16, near[2][0]),
            (Y0, Y0, 16, near[2][1]),
        ):
            result.append(
                pltpu.make_async_remote_copy(
                    send.at[slot, pl.ds(src, size), :],
                    recv.at[slot, pl.ds(dst, size), :],
                    send_sem,
                    recv_sem.at[slot],
                    device_id=where,
                    device_id_type=pl.DeviceIdType.MESH,
                )
            )
        return result

    def datum(inner, outer):
        return (inner - (1.0 - ROBIN) * outer) * SHARE

    def emit(slot, row, packed):
        moves = copies(slot)
        moves[0].start()
        moves[1].start()
        for tr in range(2):
            base = plane(row, tr, 0)

            def xrow(i):
                return u[pl.ds(base + i, CZ, stride=PAD), :]

            send[slot, pl.ds(X0 + 8 * tr, 8), :] = datum(xrow(1), xrow(0))
            send[slot, pl.ds(X1 + 8 * tr, 8), :] = datum(xrow(CX - 2), xrow(CX - 1))
            p = packed[tr]
            mixed = jnp.where(place == 0, datum(p, pltpu.roll(p, CY - 1, 1)), datum(p, pltpu.roll(p, 1, 1)))
            send[slot, pl.ds(Y0 + 8 * tr, 8), :] = mixed
        for m in moves[2:]:
            m.start()

    def gather_sends(slot, cells, packed, xt, z, field):
        for tr in range(2):
            if z == 1:
                send[slot, pl.ds(Z0 + CX * tr + 8 * xt, 8), :] = datum(field[tr, 1], field[tr, 0])
            if z == CZ - 1:
                send[slot, pl.ds(Z1 + CX * tr + 8 * xt, 8), :] = datum(field[tr, CZ - 2], field[tr, CZ - 1])
            k = z * XT + xt
            packed[tr] = jnp.where(group == k, pltpu.roll(cells[tr], (4 * k + 2) % CY, 1), packed[tr])

    packed = [zero, zero]
    for xt in range(XT):
        field = {}
        for z in range(CZ):
            cells = [dense[tr, z, pl.ds(8 * xt, 8), :] for tr in range(2)]
            for tr in range(2):
                u[pl.ds(plane(0, tr, z) + 8 * xt, 8), :] = cells[tr]
                field[tr, z] = cells[tr]
            gather_sends(0, cells, packed, xt, z, field)
    emit(0, 0, packed)

    get_speed.wait()
    get_rates.wait()
    get_region.wait()
    f = flags[0, 0, 0]
    against = [((f // (2**d)) % 2).astype(jnp.float32) for d in range(3)]
    for z in range(CZ):
        for xt in range(XT):
            at = pl.ds(z * CX + 8 * xt, 8)
            cell = pl.ds(8 * xt, 8)
            s = [raw[d, z, cell, :] for d in range(3)]
            low, high = [], []
            for d, ref in enumerate((az, ax, ay)):
                up = s[d] * against[d]
                low.append(DIFFUSE + (s[d] - up))
                high.append(DIFFUSE + up)
                ref[0, at, :] = low[d]
                ref[1, at, :] = high[d]
            own = jnp.where(first, low[2], 0.0) + jnp.where(last, high[2], 0.0)
            if z == 0:
                own = own + low[0]
            if z == CZ - 1:
                own = own + high[0]
            if xt == 0:
                own = own + jnp.where(sub == 0, low[1], 0.0)
            if xt == XT - 1:
                own = own + jnp.where(sub == 7, high[1], 0.0)
            centre = (1.0 - 6.0 * DIFFUSE) - ((s[0] + s[1]) + s[2])
            cc[0, at, :] = centre + own
            cc[1, at, :] = centre + own * SHARE
            react = zone[z, cell, :].astype(jnp.float32)
            kk[0, at, :] = react * raw[3, z, cell, :]
            kk[1, at, :] = react * raw[4, z, cell, :]

    def update(src, dst, slot, to_slot):
        which = 0 if slot is None else 1
        if slot is not None:
            mixed = []
            for tr in range(2):
                base = plane(src, tr, 0)
                u[pl.ds(base - 1, CZ, stride=PAD), :] = recv[slot, pl.ds(X0 + 8 * tr, 8), :]
                u[pl.ds(base + CX, CZ, stride=PAD), :] = recv[slot, pl.ds(X1 + 8 * tr, 8), :]
                from_low = recv[slot, pl.ds(Y0 + 8 * tr, 8), :]
                from_high = recv[slot, pl.ds(Y1 + 8 * tr, 8), :]
                mixed.append(jnp.where(place == 0, from_low, pltpu.roll(from_high, CY - 4, 1)))
        packed = [zero, zero]
        for xt in range(XT):
            now = {}
            field = {}
            for z in range(CZ):
                at = pl.ds(z * CX + 8 * xt, 8)
                k = z * XT + xt
                for tr in range(2):
                    for zz in (z, z + 1):
                        if zz < CZ and (tr, zz) not in now:
                            now[tr, zz] = u[pl.ds(plane(src, tr, zz) + 8 * xt, 8), :]
                coef = [az[0, at, :], az[1, at, :], ax[0, at, :], ax[1, at, :], ay[0, at, :], ay[1, at, :]]
                centre = cc[which, at, :]
                react = kk[1, at, :] * now[1, z] - kk[0, at, :] * now[0, z]
                cells = []
                for tr in range(2):
                    c = now[tr, z]
                    base = plane(src, tr, z) + 8 * xt
                    y_low = pltpu.roll(c, 1, 1)
                    y_high = pltpu.roll(c, CY - 1, 1)
                    if slot is None:
                        y_low = jnp.where(first, 0.0, y_low)
                        y_high = jnp.where(last, 0.0, y_high)
                    else:
                        ghost = pltpu.roll(mixed[tr], (CY - 4 * k) % CY, 1) if k else mixed[tr]
                        y_low = jnp.where(first, ghost, y_low)
                        y_high = jnp.where(last, ghost, y_high)
                    total = coef[4] * y_low + coef[5] * y_high
                    total = total + (coef[2] * u[pl.ds(base - 1, 8), :] + coef[3] * u[pl.ds(base + 1, 8), :])
                    z_low = now.get((tr, z - 1))
                    z_high = now.get((tr, z + 1))
                    if slot is not None:
                        if z == 0:
                            z_low = recv[slot, pl.ds(Z0 + CX * tr + 8 * xt, 8), :]
                        if z == CZ - 1:
                            z_high = recv[slot, pl.ds(Z1 + CX * tr + 8 * xt, 8), :]
                    if z_low is not None:
                        total = total + coef[0] * z_low
                    if z_high is not None:
                        total = total + coef[1] * z_high
                    total = total + centre * c
                    new = total + react if tr == 0 else total - react
                    u[pl.ds(plane(dst, tr, z) + 8 * xt, 8), :] = new
                    cells.append(new)
                    field[tr, z] = new
                if to_slot is not None:
                    gather_sends(to_slot, cells, packed, xt, z, field)
        if to_slot is not None:
            emit(to_slot, dst, packed)

    def rows(t):
        source = ((t + 15) // 16) * (1 + (t + 1) % 2)
        return pl.multiple_of(source * FIELD, 8), pl.multiple_of((1 + t % 2) * FIELD, 8)

    def wait_slot(slot):
        whole = recv.at[slot]
        pltpu.make_async_copy(whole, whole, recv_sem.at[slot]).wait()

    @pl.loop(0, NT - 2)
    def _(t):
        src, dst = rows(t)
        update(src, dst, None, t + 1)

    @pl.loop(0, NT - 1)
    def _(t):
        src, dst = rows(t)
        wait_slot(t)
        update(src, dst, t, NT - 1 + t)

    src, dst = rows(0)
    update(0, FIELD, 0, None)

    @pl.loop(1, NT)
    def _(t):
        src, dst = rows(t)
        wait_slot(NT - 2 + t)
        update(src, dst, NT - 2 + t, None)

    final = (1 + (NT - 1) % 2) * FIELD
    for tr in range(2):
        for z in range(CZ):
            dense[tr, z] = u[pl.ds(plane(final, tr, z), CX), :]
    put = pltpu.make_async_copy(dense, out, out_sem)
    put.start()
    pltpu.make_async_copy(send, send, send_sem).wait()
    put.wait()


def body(conc, speed, rates, region, flow_signs):
    hbm = pl.BlockSpec(memory_space=pltpu.HBM)
    f32 = jnp.float32
    return pl.pallas_call(
        kernel,
        out_shape=jax.ShapeDtypeStruct(conc.shape, f32),
        in_specs=[hbm, hbm, hbm, hbm, pl.BlockSpec(memory_space=pltpu.SMEM)],
        out_specs=hbm,
        scratch_shapes=[
            pltpu.VMEM((3 * FIELD, CY), f32),
            pltpu.VMEM((2, CZ, CX, CY), f32),
            pltpu.VMEM((5, CZ, CX, CY), f32),
            pltpu.VMEM((CZ, CX, CY), jnp.int32),
            pltpu.VMEM((2, CZ * CX, CY), f32),
            pltpu.VMEM((2, CZ * CX, CY), f32),
            pltpu.VMEM((2, CZ * CX, CY), f32),
            pltpu.VMEM((2, CZ * CX, CY), f32),
            pltpu.VMEM((2, CZ * CX, CY), f32),
            pltpu.VMEM((SLOTS, SLOT, CY), f32),
            pltpu.VMEM((SLOTS, SLOT, CY), f32),
            pltpu.SemaphoreType.DMA((4,)),
            pltpu.SemaphoreType.DMA,
            pltpu.SemaphoreType.DMA,
            pltpu.SemaphoreType.DMA((SLOTS,)),
        ],
        compiler_params=pltpu.CompilerParams(
            collective_id=0, has_side_effects=True, vmem_limit_bytes=32 * 1024 * 1024
        ),
    )(conc, speed, rates, region, flow_signs)


def solution(mesh):
    placed = (
        P(None, "gz", "gx", "gy"),
        P(None, "gz", "gx", "gy"),
        P(None, "gz", "gx", "gy"),
        P("gz", "gx", "gy"),
        P("gz", "gx", "gy"),
    )
    return jax.shard_map(
        body, mesh=mesh, in_specs=placed, out_specs=P(None, "gz", "gx", "gy"), check_vma=False
    )
```

```python
import functools

import jax
import jax.numpy as jnp
from jax import lax
from jax.experimental import pallas as pl
from jax.experimental.pallas import tpu as pltpu
from jax.sharding import PartitionSpec as P

NT = 16
ROBIN = 0.5
DIFFUSE = 0.07
SHARE = 1.0 / (1.0 + ROBIN)

CZ, CX, CY = 8, 32, 128
XT = CX // 8
PAD = CX + 16
FIELD = 2 * CZ * PAD
AXES = ("gz", "gx", "gy")
Z0, Z1, X0, X1, Y0, Y1, SLOT = 0, 64, 128, 144, 160, 176, 192
SLOTS = 2 * (NT - 1)


def kernel(conc, speed, rates, region, flags, out, ua, ub, dense, raw, zone, az, ax, ay, cc, kk, send, recv, in_sem, out_sem, send_sem, recv_sem):
    def plane(tr, z):
        return (tr * CZ + z) * PAD + 8

    get_conc = pltpu.make_async_copy(conc, dense, in_sem.at[0])
    get_conc.start()
    get_speed = pltpu.make_async_copy(speed, raw.at[pl.ds(0, 3)], in_sem.at[1])
    get_rates = pltpu.make_async_copy(rates, raw.at[pl.ds(3, 2)], in_sem.at[2])
    get_region = pltpu.make_async_copy(region, zone, in_sem.at[3])
    get_speed.start()
    get_rates.start()
    get_region.start()

    near = []
    for name in AXES:
        n, me = lax.axis_size(name), lax.axis_index(name)
        near.append(({name: lax.rem(me + n - 1, n)}, {name: lax.rem(me + 1, n)}))
    barrier = pltpu.get_barrier_semaphore()
    for low, high in near:
        pl.semaphore_signal(barrier, inc=1, device_id=low, device_id_type=pl.DeviceIdType.MESH)
        pl.semaphore_signal(barrier, inc=1, device_id=high, device_id_type=pl.DeviceIdType.MESH)

    zero = jnp.zeros((8, CY), jnp.float32)
    for u in (ua, ub):
        for tr in range(2):
            for z in range(CZ):
                u[pl.ds(plane(tr, z) - 8, 8), :] = zero
                u[pl.ds(plane(tr, z) + CX, 8), :] = zero

    lane = lax.broadcasted_iota(jnp.int32, (8, CY), 1)
    sub = lax.broadcasted_iota(jnp.int32, (8, CY), 0)
    first, last = lane == 0, lane == CY - 1
    group, place = lane // 4, lane % 4

    get_conc.wait()
    pl.semaphore_wait(barrier, 6)

    def copies(slot):
        result = []
        for src, dst, size, where in (
            (Z0, Z1, 64, near[0][0]),
            (Z1, Z0, 64, near[0][1]),
            (X0, X1, 16, near[1][0]),
            (X1, X0, 16, near[1][1]),
            (Y0, Y1, 16, near[2][0]),
            (Y0, Y0, 16, near[2][1]),
        ):
            result.append(
                pltpu.make_async_remote_copy(
                    send.at[slot, pl.ds(src, size), :],
                    recv.at[slot, pl.ds(dst, size), :],
                    send_sem,
                    recv_sem.at[slot],
                    device_id=where,
                    device_id_type=pl.DeviceIdType.MESH,
                )
            )
        return result

    def datum(inner, outer):
        return (inner - (1.0 - ROBIN) * outer) * SHARE

    def emit(slot, u, packed):
        moves = copies(slot)
        moves[0].start()
        moves[1].start()
        for tr in range(2):
            base = plane(tr, 0)

            def xrow(i):
                return u[pl.ds(base + i, CZ, stride=PAD), :]

            send[slot, pl.ds(X0 + 8 * tr, 8), :] = datum(xrow(1), xrow(0))
            send[slot, pl.ds(X1 + 8 * tr, 8), :] = datum(xrow(CX - 2), xrow(CX - 1))
            p = packed[tr]
            mixed = jnp.where(place == 0, datum(p, pltpu.roll(p, CY - 1, 1)), datum(p, pltpu.roll(p, 1, 1)))
            send[slot, pl.ds(Y0 + 8 * tr, 8), :] = mixed
        for m in moves[2:]:
            m.start()

    def gather_sends(slot, cells, packed, xt, z, field):
        for tr in range(2):
            if z == 1:
                send[slot, pl.ds(Z0 + CX * tr + 8 * xt, 8), :] = datum(field[tr, 1], field[tr, 0])
            if z == CZ - 1:
                send[slot, pl.ds(Z1 + CX * tr + 8 * xt, 8), :] = datum(field[tr, CZ - 2], field[tr, CZ - 1])
            k = z * XT + xt
            packed[tr] = jnp.where(group == k, pltpu.roll(cells[tr], (4 * k + 2) % CY, 1), packed[tr])

    packed = [zero, zero]
    for xt in range(XT):
        field = {}
        for z in range(CZ):
            cells = [dense[tr, z, pl.ds(8 * xt, 8), :] for tr in range(2)]
            for tr in range(2):
                ua[pl.ds(plane(tr, z) + 8 * xt, 8), :] = cells[tr]
                field[tr, z] = cells[tr]
            gather_sends(0, cells, packed, xt, z, field)
    emit(0, ua, packed)

    get_speed.wait()
    get_rates.wait()
    get_region.wait()
    f = flags[0, 0, 0]
    against = [((f // (2**d)) % 2).astype(jnp.float32) for d in range(3)]
    for z in range(CZ):
        for xt in range(XT):
            at = pl.ds(z * CX + 8 * xt, 8)
            cell = pl.ds(8 * xt, 8)
            s = [raw[d, z, cell, :] for d in range(3)]
            low, high = [], []
            for d, ref in enumerate((az, ax, ay)):
                up = s[d] * against[d]
                low.append(DIFFUSE + (s[d] - up))
                high.append(DIFFUSE + up)
                ref[0, at, :] = low[d]
                ref[1, at, :] = high[d]
            own = jnp.where(first, low[2], 0.0) + jnp.where(last, high[2], 0.0)
            if z == 0:
                own = own + low[0]
            if z == CZ - 1:
                own = own + high[0]
            if xt == 0:
                own = own + jnp.where(sub == 0, low[1], 0.0)
            if xt == XT - 1:
                own = own + jnp.where(sub == 7, high[1], 0.0)
            centre = (1.0 - 6.0 * DIFFUSE) - ((s[0] + s[1]) + s[2])
            cc[0, at, :] = centre + own
            cc[1, at, :] = centre + own * SHARE
            react = zone[z, cell, :].astype(jnp.float32)
            kk[0, at, :] = react * raw[3, z, cell, :]
            kk[1, at, :] = react * raw[4, z, cell, :]

    def update(src, dst, slot, to_slot):
        which = 0 if slot is None else 1
        if slot is not None:
            mixed = []
            for tr in range(2):
                base = plane(tr, 0)
                src[pl.ds(base - 1, CZ, stride=PAD), :] = recv[slot, pl.ds(X0 + 8 * tr, 8), :]
                src[pl.ds(base + CX, CZ, stride=PAD), :] = recv[slot, pl.ds(X1 + 8 * tr, 8), :]
                from_low = recv[slot, pl.ds(Y0 + 8 * tr, 8), :]
                from_high = recv[slot, pl.ds(Y1 + 8 * tr, 8), :]
                mixed.append(jnp.where(place == 0, from_low, pltpu.roll(from_high, CY - 4, 1)))
        packed = [zero, zero]
        for xt in range(XT):
            now = {}
            field = {}
            for z in range(CZ):
                at = pl.ds(z * CX + 8 * xt, 8)
                k = z * XT + xt
                for tr in range(2):
                    for zz in (z, z + 1):
                        if zz < CZ and (tr, zz) not in now:
                            now[tr, zz] = src[pl.ds(plane(tr, zz) + 8 * xt, 8), :]
                coef = [az[0, at, :], az[1, at, :], ax[0, at, :], ax[1, at, :], ay[0, at, :], ay[1, at, :]]
                centre = cc[which, at, :]
                react = kk[1, at, :] * now[1, z] - kk[0, at, :] * now[0, z]
                cells = []
                for tr in range(2):
                    c = now[tr, z]
                    base = plane(tr, z) + 8 * xt
                    y_low = pltpu.roll(c, 1, 1)
                    y_high = pltpu.roll(c, CY - 1, 1)
                    if slot is None:
                        y_low = jnp.where(first, 0.0, y_low)
                        y_high = jnp.where(last, 0.0, y_high)
                    else:
                        ghost = pltpu.roll(mixed[tr], (CY - 4 * k) % CY, 1) if k else mixed[tr]
                        y_low = jnp.where(first, ghost, y_low)
                        y_high = jnp.where(last, ghost, y_high)
                    total = coef[4] * y_low + coef[5] * y_high
                    total = total + (coef[2] * src[pl.ds(base - 1, 8), :] + coef[3] * src[pl.ds(base + 1, 8), :])
                    z_low = now.get((tr, z - 1))
                    z_high = now.get((tr, z + 1))
                    if slot is not None:
                        if z == 0:
                            z_low = recv[slot, pl.ds(Z0 + CX * tr + 8 * xt, 8), :]
                        if z == CZ - 1:
                            z_high = recv[slot, pl.ds(Z1 + CX * tr + 8 * xt, 8), :]
                    if z_low is not None:
                        total = total + coef[0] * z_low
                    if z_high is not None:
                        total = total + coef[1] * z_high
                    total = total + centre * c
                    new = total + react if tr == 0 else total - react
                    dst[pl.ds(base, 8), :] = new
                    cells.append(new)
                    field[tr, z] = new
                if to_slot is not None:
                    gather_sends(to_slot, cells, packed, xt, z, field)
        if to_slot is not None:
            emit(to_slot, dst, packed)

    def step(slot, to_slot):
        update(ua, ub, slot, to_slot)
        for tr in range(2):
            for z in range(CZ):
                ua[pl.ds(plane(tr, z), CX), :] = ub[pl.ds(plane(tr, z), CX), :]

    def restart():
        for tr in range(2):
            for z in range(CZ):
                ua[pl.ds(plane(tr, z), CX), :] = dense[tr, z]

    def wait_slot(slot):
        whole = recv.at[slot]
        pltpu.make_async_copy(whole, whole, recv_sem.at[slot]).wait()

    @pl.loop(0, NT - 2)
    def _(t):
        step(None, t + 1)

    restart()

    @pl.loop(0, NT - 1)
    def _(t):
        wait_slot(t)
        step(t, NT - 1 + t)

    restart()

    @pl.loop(0, NT)
    def _(t):
        @pl.when(t > 0)
        def _():
            wait_slot(NT - 2 + t)

        step(((t + NT - 1) // NT) * (NT - 2 + t), None)

    for tr in range(2):
        for z in range(CZ):
            dense[tr, z] = ua[pl.ds(plane(tr, z), CX), :]
    put = pltpu.make_async_copy(dense, out, out_sem)
    put.start()
    pltpu.make_async_copy(send, send, send_sem).wait()
    put.wait()


def body(conc, speed, rates, region, flow_signs):
    hbm = pl.BlockSpec(memory_space=pltpu.HBM)
    f32 = jnp.float32
    return pl.pallas_call(
        kernel,
        out_shape=jax.ShapeDtypeStruct(conc.shape, f32),
        in_specs=[hbm, hbm, hbm, hbm, pl.BlockSpec(memory_space=pltpu.SMEM)],
        out_specs=hbm,
        scratch_shapes=[
            pltpu.VMEM((FIELD, CY), f32),
            pltpu.VMEM((FIELD, CY), f32),
            pltpu.VMEM((2, CZ, CX, CY), f32),
            pltpu.VMEM((5, CZ, CX, CY), f32),
            pltpu.VMEM((CZ, CX, CY), jnp.int32),
            pltpu.VMEM((2, CZ * CX, CY), f32),
            pltpu.VMEM((2, CZ * CX, CY), f32),
            pltpu.VMEM((2, CZ * CX, CY), f32),
            pltpu.VMEM((2, CZ * CX, CY), f32),
            pltpu.VMEM((2, CZ * CX, CY), f32),
            pltpu.VMEM((SLOTS, SLOT, CY), f32),
            pltpu.VMEM((SLOTS, SLOT, CY), f32),
            pltpu.SemaphoreType.DMA((4,)),
            pltpu.SemaphoreType.DMA,
            pltpu.SemaphoreType.DMA,
            pltpu.SemaphoreType.DMA((SLOTS,)),
        ],
        compiler_params=pltpu.CompilerParams(
            collective_id=0, has_side_effects=True, vmem_limit_bytes=60 * 1024 * 1024
        ),
    )(conc, speed, rates, region, flow_signs)


def solution(mesh):
    placed = (
        P(None, "gz", "gx", "gy"),
        P(None, "gz", "gx", "gy"),
        P(None, "gz", "gx", "gy"),
        P("gz", "gx", "gy"),
        P("gz", "gx", "gy"),
    )
    return jax.shard_map(
        body, mesh=mesh, in_specs=placed, out_specs=P(None, "gz", "gx", "gy"), check_vma=False
    )
```
